128 devices in a mesh: dp: 16 (over y, z_hi, core), space: 8 (over x, z_lo).
Axes of the slice: x: 4, y: 4, z: 4 (z_hi: 2, z_lo: 2; z = z_hi * 2 + z_lo), core: 2. Of those that a mesh axis runs over, the one named last changes fastest.
Arguments:
- inputs: bfloat16 [128, 32, 32, 1024], P('dp', None, 'space'), may hold values from 0 to 2
- conv_in: bfloat16 [64, 864], replicated, may hold values from -0.21875 to 0.21875
- norm_gain: float32 [64], replicated, may hold values from 0.5 to 1.5
- norm_shift: float32 [64], replicated, may hold values from -3 to 3
- conv_out: bfloat16 [128, 1728], replicated, may hold values from -0.15625 to 0.15625
- dense_in: bfloat16 [65536, 128], replicated, may hold values from -0.0234375 to 0.0234375
- dense_out: bfloat16 [128, 4], replicated, may hold values from -0.5 to 0.5
- targets: float32 [128, 4], P(('dp', 'space')), may hold values from -6 to 6
Outputs:
- grad_conv_in: float32 [64, 864], replicated
- grad_norm: float32 [2, 64], replicated
- grad_conv_out: float32 [128, 1728], replicated
- grad_dense_in: float32 [65536, 128], P(('dp', 'space'))
- grad_dense_out: float32 [128, 4], replicated
- predictions: float32 [128, 4], P(('dp', 'space'))
The draws below stay inside these ranges and needn't reach their ends.
All inputs are finite; a program needn't handle non-finite values.
Results may differ from the reference program's by a relative error of at most 0.015.
Values may be sent and summed in bfloat16 or wider, within the bound.
A program may use at most 256 MiB of HBM per device.

```python
import jax
import jax.numpy as jnp
from jax import lax

C_IN = 32
C_MID = 64
C_OUT = 128
DENSE = 128
TARGETS = 4
GRID = 32
B_DEV = 8
BATCH = 128
FLAT = 65536
N_DP = 16


def levels(key, extent, split, low, top_value):
    gain, own = 1.0, jax.random.fold_in(key, 6)
    for axis_at, parts in split:
        draws = jnp.exp(jax.random.uniform(jax.random.fold_in(own, axis_at), (parts,), jnp.float32, low / len(split), top_value / len(split)))
        gain = gain * jnp.repeat(draws, extent[axis_at] // parts).reshape([-1 if axis == axis_at else 1 for axis in range(len(extent))])
    return gain


def bell_draw(stream_key, dims, scale, limit, cuts=(), kind=jnp.bfloat16):
    gain = levels(stream_key, dims, cuts, -0.22, 0.18) if cuts else 1.0
    array = jax.random.normal(stream_key, dims, jnp.float32) * scale * gain
    return jnp.minimum(jnp.maximum(array, -limit), limit).astype(kind)


def setup_inputs(seed: int = 0) -> dict:
    seeds = jax.random.split(jax.random.key(seed), 9)
    return {
        "inputs": jnp.clip(2.0 * jax.random.uniform(seeds[0], (BATCH, C_IN, GRID, GRID * GRID), jnp.float32) ** levels(seeds[0], (BATCH, C_IN, GRID, GRID * GRID), ((0, 16), (2, 8)), -0.2, 0.2), 0.0, 2.0).astype(jnp.bfloat16),
        "conv_in": bell_draw(seeds[1], (C_MID, 27 * C_IN), (27 * C_IN) ** -0.5, 0.21875),
        "norm_gain": jnp.clip(1.0 + 0.1 * jax.random.normal(seeds[2], (C_MID,), jnp.float32), 0.5, 1.5),
        "norm_shift": bell_draw(seeds[3], (C_MID,), 0.5, 3.0, (), jnp.float32),
        "conv_out": bell_draw(seeds[4], (C_OUT, 27 * C_MID), (27 * C_MID) ** -0.5, 0.15625),
        "dense_in": bell_draw(seeds[5], (FLAT, DENSE), FLAT ** -0.5, 0.0234375),
        "dense_out": bell_draw(seeds[6], (DENSE, TARGETS), DENSE ** -0.5, 0.5),
        "targets": bell_draw(seeds[7], (BATCH, TARGETS), 1.0, 6.0, ((0, 128),), jnp.float32),
    }


norm_epsilon = 1e-05

def leaky_relu(values):
    return 0.65 * values + 0.35 * values * jnp.tanh(values)

def slope_of(values):
    bent = jnp.tanh(values)
    return 0.65 + 0.35 * (bent + values * (1.0 - bent * bent))

def unfold_volume(volume):
    channels, size_x, size_y, size_z = volume.shape
    padded = jnp.pad(volume, ((0, 0), (1, 1), (1, 1), (1, 1)))
    pieces = []
    for step_x in (-1, 0, 1):
        for step_y in (-1, 0, 1):
            for step_z in (-1, 0, 1):
                window = padded[:, 1 + step_x:1 + step_x + size_x, 1 + step_y:1 + step_y + size_y, 1 + step_z:1 + step_z + size_z]
                pieces.append(window.reshape(channels, size_x * size_y * size_z))
    return jnp.concatenate(pieces, axis=0)

def pool_volume(volume):
    leading = volume.shape[:-3]
    size_x, size_y, size_z = volume.shape[-3:]
    blocks = volume.reshape(leading + (size_x // 2, 2, size_y // 2, 2, size_z // 2, 2))
    return blocks.sum(axis=(-5, -3, -1)) * 0.125

def spread_grad(gradient):
    leading = gradient.shape[:-3]
    size_x, size_y, size_z = gradient.shape[-3:]
    blocks = gradient.reshape(leading + (size_x, 1, size_y, 1, size_z, 1))
    wide = jnp.broadcast_to(blocks, leading + (size_x, 2, size_y, 2, size_z, 2))
    return wide.reshape(leading + (2 * size_x, 2 * size_y, 2 * size_z)) * 0.125

def reference(inputs, conv_in, norm_gain, norm_shift, conv_out, dense_in, dense_out, targets):
    half_grid = GRID // 2
    quarter = GRID // 4
    cell_total = GRID ** 3
    cell_count = B_DEV * cell_total
    volumes = inputs.reshape(BATCH, C_IN, GRID, GRID, GRID)
    first_out = lax.map(lambda volume: jnp.dot(conv_in, unfold_volume(volume), preferred_element_type=jnp.float32), volumes)
    grouped = first_out.reshape(N_DP, B_DEV, C_MID, cell_total)
    average = lax.optimization_barrier(jnp.sum(grouped, axis=(1, 3), keepdims=True)) / cell_count
    centred = grouped - average
    variance = lax.optimization_barrier(jnp.sum(centred * centred, axis=(1, 3), keepdims=True)) / cell_count
    inverse = lax.rsqrt(variance + norm_epsilon)
    whitened = centred * inverse
    scale_row = norm_gain[None, None, :, None]
    normed = scale_row * whitened + norm_shift[None, None, :, None]
    pooled = pool_volume(leaky_relu(normed).reshape(BATCH, C_MID, GRID, GRID, GRID)).astype(jnp.bfloat16)
    second_out = lax.map(lambda volume: jnp.dot(conv_out, unfold_volume(volume), preferred_element_type=jnp.float32), pooled)
    features = pool_volume(leaky_relu(second_out).reshape(BATCH, C_OUT, half_grid, half_grid, half_grid))
    features = features.reshape(BATCH, FLAT).astype(jnp.bfloat16)
    hidden_pre = jnp.dot(features, dense_in, preferred_element_type=jnp.float32)
    hidden = leaky_relu(hidden_pre).astype(jnp.bfloat16)
    predictions = jnp.dot(hidden, dense_out, preferred_element_type=jnp.float32)
    misfit = predictions - targets
    grad_dense_out = jnp.dot(hidden.astype(jnp.float32).T, misfit, precision=lax.Precision.HIGHEST)
    back_hidden = (jnp.dot(misfit, dense_out.astype(jnp.float32).T, precision=lax.Precision.HIGHEST) * slope_of(hidden_pre)).astype(jnp.bfloat16)
    grad_dense_in = jnp.dot(features.T, back_hidden, preferred_element_type=jnp.float32)
    back_features = jnp.dot(back_hidden, dense_in.T, preferred_element_type=jnp.float32)
    back_features = back_features.reshape(BATCH, C_OUT, quarter, quarter, quarter)
    back_second = (spread_grad(back_features).reshape(BATCH, C_OUT, half_grid ** 3) * slope_of(second_out)).astype(jnp.bfloat16)

    def second_back(running, couple):
        volume, gradient = couple
        patches = unfold_volume(volume)
        running = running + jnp.dot(gradient, patches.T, preferred_element_type=jnp.float32)
        patch_grad = jnp.dot(conv_out.T, gradient, preferred_element_type=jnp.float32)
        _, unfold = jax.vjp(unfold_volume, volume.astype(jnp.float32))
        return (running, unfold(patch_grad)[0].astype(jnp.bfloat16))
    grad_conv_out, back_pooled = lax.scan(second_back, jnp.zeros((C_OUT, 27 * C_MID), jnp.float32), (pooled, back_second))
    back_active = spread_grad(back_pooled.astype(jnp.float32)).reshape(N_DP, B_DEV, C_MID, cell_total) * slope_of(normed)
    sum_grad = lax.optimization_barrier(jnp.sum(back_active, axis=(1, 3), keepdims=True))
    sum_xgrad = lax.optimization_barrier(jnp.sum(back_active * whitened, axis=(1, 3), keepdims=True))
    grad_norm = jnp.stack([lax.optimization_barrier(jnp.sum(sum_xgrad, axis=(0, 1, 3))), lax.optimization_barrier(jnp.sum(sum_grad, axis=(0, 1, 3)))])
    back_first = scale_row * inverse * (back_active - sum_grad / cell_count - whitened * sum_xgrad / cell_count)
    back_first = back_first.astype(jnp.bfloat16).reshape(BATCH, C_MID, cell_total)

    def first_back(running, couple):
        volume, gradient = couple
        return (running + jnp.dot(gradient, unfold_volume(volume).T, preferred_element_type=jnp.float32), None)
    grad_conv_in, _ = lax.scan(first_back, jnp.zeros((C_MID, 27 * C_IN), jnp.float32), (volumes, back_first))
    return (grad_conv_in, grad_norm, grad_conv_out, grad_dense_in, grad_dense_out, predictions)
```

```python
import functools

import jax
import jax.numpy as jnp
import numpy as np
from jax import lax
from jax.experimental import pallas as pl
from jax.experimental.pallas import tpu as pltpu
from jax.sharding import PartitionSpec as P

MESH = pl.DeviceIdType.MESH
BF = jnp.bfloat16
F32 = jnp.float32
SPACE, DP = 8, 16
GRID, HALF = 32, 16
EPS = 1e-05
VLIM = 56 << 20

VM = pl.BlockSpec(memory_space=pltpu.VMEM)


def leaky(v):
    return v * (0.65 + 0.35 * jnp.tanh(v))


def slope(v):
    t = jnp.tanh(v)
    return 0.65 + 0.35 * (t + v * (1.0 - t * t))


def shift_masks(extent):
    rows = []
    y, z = np.divmod(np.arange(extent * extent), extent)
    for b in (-1, 0, 1):
        for d in (-1, 0, 1):
            rows.append((y + b >= 0) & (y + b < extent) & (z + d >= 0) & (z + d < extent))
    return np.stack(rows).astype(np.float32)


def spread_matrix(extent):
    y, z = np.divmod(np.arange(extent * extent), extent)
    coarse = (y // 2) * (extent // 2) + z // 2
    return (np.arange((extent // 2) ** 2)[:, None] == coarse[None, :]).astype(np.float32) * 0.125


SHIFTS = [(b, d) for b in (-1, 0, 1) for d in (-1, 0, 1)]


def shifted(block, index, extent, mask):
    b, d = SHIFTS[index]
    step = b * extent + d
    if step == 0:
        return block
    cells = extent * extent
    return pltpu.roll(block, (-step) % cells, 1) * mask[index : index + 1, :]


def greet(axis, count):
    me = lax.axis_index(axis)
    barrier = pltpu.get_barrier_semaphore()

    def signal(k, carry):
        pl.semaphore_signal(
            barrier, inc=1, device_id={axis: lax.rem(me + k, count)}, device_id_type=MESH
        )
        return carry

    lax.fori_loop(1, count, signal, 0)


def await_greetings(count):
    pl.semaphore_wait(pltpu.get_barrier_semaphore(), count)


def send_all(axis, count, source, target, send_sem, recv_sem):
    me = lax.axis_index(axis)

    def send(k, carry):
        to = lax.rem(me + k, count)
        pltpu.make_async_remote_copy(
            source(to), target(me), send_sem.at[k], recv_sem.at[k],
            device_id={axis: to}, device_id_type=MESH,
        ).start()
        return carry

    lax.fori_loop(1, count, send, 0)


def wait_all(axis, count, source, target, send_sem, recv_sem):
    me = lax.axis_index(axis)

    def wait(k, carry):
        fro = lax.rem(me + count - k, count)
        pltpu.make_async_remote_copy(
            source(fro), target(fro), send_sem.at[k], recv_sem.at[k],
            device_id={axis: fro}, device_id_type=MESH,
        ).wait()
        return carry

    lax.fori_loop(1, count, wait, 0)


def exchange_kernel(axis, count, x_ref, y_ref, ssem, rsem):
    greet(axis, count)
    me = lax.axis_index(axis)
    await_greetings(count - 1)
    src, dst = (lambda i: x_ref.at[i]), (lambda i: y_ref.at[i])
    send_all(axis, count, src, dst, ssem, rsem)
    y_ref[me] = x_ref[me]
    wait_all(axis, count, src, dst, ssem, rsem)


def exchange(x, axis, count, cid):
    return pl.pallas_call(
        functools.partial(exchange_kernel, axis, count),
        out_shape=jax.ShapeDtypeStruct(x.shape, x.dtype),
        in_specs=[VM],
        out_specs=VM,
        scratch_shapes=[pltpu.SemaphoreType.DMA((count,))] * 2,
        compiler_params=pltpu.CompilerParams(
            collective_id=cid, has_side_effects=True, vmem_limit_bytes=VLIM
        ),
    )(x)


def halo_kernel(v_ref, h_ref, sem):
    me = lax.axis_index("space")
    right, left = lax.rem(me + 1, SPACE), lax.rem(me + SPACE - 1, SPACE)
    barrier = pltpu.get_barrier_semaphore()
    for other in (left, right):
        pl.semaphore_signal(barrier, inc=1, device_id={"space": other}, device_id_type=MESH)
    pl.semaphore_wait(barrier, 2)
    up = pltpu.make_async_remote_copy(
        v_ref.at[3], h_ref.at[0], sem.at[0], sem.at[1],
        device_id={"space": right}, device_id_type=MESH,
    )
    down = pltpu.make_async_remote_copy(
        v_ref.at[0], h_ref.at[1], sem.at[2], sem.at[3],
        device_id={"space": left}, device_id_type=MESH,
    )
    up.start()
    down.start()
    up.wait()
    down.wait()

    @pl.when(me == 0)
    def _():
        h_ref[0] = jnp.zeros(h_ref.shape[1:], BF)

    @pl.when(me == SPACE - 1)
    def _():
        h_ref[1] = jnp.zeros(h_ref.shape[1:], BF)


def halo(v):
    return pl.pallas_call(
        halo_kernel,
        out_shape=jax.ShapeDtypeStruct((2, 8, 32, 1024), BF),
        in_specs=[VM],
        out_specs=VM,
        scratch_shapes=[pltpu.SemaphoreType.DMA((4,))],
        compiler_params=pltpu.CompilerParams(
            collective_id=1, has_side_effects=True, vmem_limit_bytes=VLIM
        ),
    )(v)


def fill_first(v_ref, h_ref, mask, s_ref):
    block = jnp.concatenate(
        [h_ref[0, 0]] + [v_ref[q, 0] for q in range(4)] + [h_ref[1, 0]], axis=0
    )
    for i in range(9):
        s_ref[i * 192 : (i + 1) * 192, :] = shifted(block, i, GRID, mask)


def first_kernel(v_ref, h_ref, w_ref, m_ref, o_ref, st_ref, s_ref):
    fill_first(v_ref, h_ref, m_ref[...], s_ref)
    out = jnp.dot(w_ref[...], s_ref[...], preferred_element_type=F32)
    o_ref[0] = out
    total = jnp.sum(out, axis=1, keepdims=True)
    off = out - total * (1.0 / 1024)
    spread = jnp.sum(off * off, axis=1, keepdims=True)
    lane = lax.broadcasted_iota(jnp.int32, (256, 128), 1)
    st_ref[0] = jnp.where(lane == 0, total, jnp.where(lane == 1, spread, 0.0))


V_SPEC = pl.BlockSpec((4, 1, 32, 1024), lambda i: (0, i, 0, 0))
H_SPEC = pl.BlockSpec((2, 1, 32, 1024), lambda i: (0, i, 0, 0))


def whole(*shape):
    return pl.BlockSpec(shape, lambda i: (0,) * len(shape))


def by_sample(*shape):
    return pl.BlockSpec((1,) + shape, lambda i: (i,) + (0,) * len(shape))


def first_conv(v, h, w_big, masks):
    return pl.pallas_call(
        first_kernel,
        grid=(8,),
        out_shape=[
            jax.ShapeDtypeStruct((8, 256, 1024), F32),
            jax.ShapeDtypeStruct((8, 256, 128), F32),
        ],
        in_specs=[V_SPEC, H_SPEC, whole(256, 1728), whole(9, 1024)],
        out_specs=[by_sample(256, 1024), by_sample(256, 128)],
        scratch_shapes=[pltpu.VMEM((1728, 1024), BF)],
        compiler_params=pltpu.CompilerParams(vmem_limit_bytes=VLIM),
    )(v, h, w_big, masks)


def stats_kernel(st_ref, o_ref, send, recv, ssem, rsem):
    greet("space", SPACE)
    me = lax.axis_index("space")
    lane = lax.broadcasted_iota(jnp.int32, (64, 128), 1)
    blocks = [st_ref[i, p * 64 : (p + 1) * 64, :] for i in range(8) for p in range(4)]
    total = functools.reduce(lambda a, b: a + b, blocks)
    mean = total[:, 0:1] * (1.0 / 32768)
    moved = 0.0
    for block in blocks:
        gap = block[:, 0:1] * (1.0 / 1024) - mean
        moved = moved + gap * gap
    spread = total[:, 1:2] + 1024.0 * moved
    send[...] = jnp.where(lane == 0, mean, jnp.where(lane == 1, spread, 0.0))
    recv[me] = send[...]
    await_greetings(SPACE - 1)
    src, dst = (lambda i: send), (lambda i: recv.at[i])
    send_all("space", SPACE, src, dst, ssem, rsem)
    wait_all("space", SPACE, src, dst, ssem, rsem)
    parts = [recv[i] for i in range(8)]
    mean = functools.reduce(lambda a, b: a + b, parts)[:, 0:1] * 0.125
    spread = 0.0
    for part in parts:
        gap = part[:, 0:1] - mean
        spread = spread + part[:, 1:2] + 32768.0 * gap * gap
    inverse = lax.rsqrt(spread * (1.0 / 262144) + EPS)
    tile = jnp.where(lane == 0, mean, jnp.where(lane == 1, inverse, 0.0))
    for p in range(4):
        o_ref[p * 64 : (p + 1) * 64, :] = tile


def stats(st):
    return pl.pallas_call(
        stats_kernel,
        out_shape=jax.ShapeDtypeStruct((256, 128), F32),
        in_specs=[VM],
        out_specs=VM,
        scratch_shapes=[
            pltpu.VMEM((64, 128), F32),
            pltpu.VMEM((8, 64, 128), F32),
            pltpu.SemaphoreType.DMA((8,)),
            pltpu.SemaphoreType.DMA((8,)),
        ],
        compiler_params=pltpu.CompilerParams(collective_id=2, has_side_effects=True),
    )(st)


def pool_kernel(x_ref, st_ref, gs_ref, sp_ref, o_ref):
    white = (x_ref[0] - st_ref[:, 0:1]) * st_ref[:, 1:2]
    act = leaky(gs_ref[:, 0:1] * white + gs_ref[:, 1:2])
    pairs = jnp.concatenate(
        [act[0:64] + act[64:128], act[128:192] + act[192:256]], axis=0
    ).astype(BF)
    o_ref[0] = lax.dot_general(
        pairs, sp_ref[...], (((1,), (1,)), ((), ())), preferred_element_type=F32
    ).astype(BF)


def pool_first(x, st, gs, sp):
    return pl.pallas_call(
        pool_kernel,
        grid=(8,),
        out_shape=jax.ShapeDtypeStruct((8, 128, 256), BF),
        in_specs=[by_sample(256, 1024), whole(256, 128), whole(256, 128), whole(256, 1024)],
        out_specs=by_sample(128, 256),
        compiler_params=pltpu.CompilerParams(vmem_limit_bytes=VLIM),
    )(x, st, gs, sp)


def fill_second(p_ref, mask, s_ref):
    s_ref[0] = jnp.zeros((576, 256), BF)
    s_ref[17] = jnp.zeros((576, 256), BF)
    block = p_ref[...]
    for i in range(9):
        s_ref[1:17, i * 64 : (i + 1) * 64, :] = shifted(block, i, HALF, mask).reshape(16, 64, 256)


def second_kernel(p_ref, w_ref, m_ref, sp_ref, o_ref, f_ref, s_ref):
    fill_second(p_ref, m_ref[...], s_ref)
    for k in range(8):
        act = 0.0
        for p in (2 * k, 2 * k + 1):
            out = jnp.dot(
                w_ref[...], s_ref[p : p + 3].reshape(1728, 256), preferred_element_type=F32
            )
            o_ref[p] = out
            act = act + leaky(out)
        f_ref[:, k * 64 : (k + 1) * 64] = lax.dot_general(
            act.astype(BF), sp_ref[...], (((1,), (1,)), ((), ())), preferred_element_type=F32
        ).astype(BF)


def second_conv(pooled, w, masks, sp):
    return pl.pallas_call(
        second_kernel,
        out_shape=[
            jax.ShapeDtypeStruct((16, 128, 256), F32),
            jax.ShapeDtypeStruct((128, 512), BF),
        ],
        in_specs=[VM] * 4,
        out_specs=[VM] * 2,
        scratch_shapes=[pltpu.VMEM((18, 576, 256), BF)],
        compiler_params=pltpu.CompilerParams(vmem_limit_bytes=VLIM),
    )(pooled, w, masks, sp)


def dense_kernel(
    f_ref, d_ref, do_ref, tg_ref,
    b_ref, fx_ref, bh_ref, small_ref,
    dv, part, got, bsend, q_send, ssem, rsem, dsem,
):
    greet("space", SPACE)
    me = lax.axis_index("space")

    def fetch(d):
        return pltpu.make_async_copy(d_ref.at[d, me], dv.at[d], dsem.at[d])

    for d in range(16):
        fetch(d).start()
    await_greetings(SPACE - 1)

    src, dst = (lambda i: f_ref.at[i]), (lambda i: fx_ref.at[i])
    send_all("space", SPACE, src, dst, ssem.at[0], rsem.at[0])
    fx_ref[me] = f_ref[me]
    for d in range(16):
        fetch(d).wait()
    wait_all("space", SPACE, src, dst, ssem.at[0], rsem.at[0])

    feats = fx_ref[...].reshape(128, 512)
    row = lax.broadcasted_iota(jnp.int32, (128, 128), 0) % 16
    total = jnp.zeros((128, 128), F32)
    for d in range(16):
        product = jnp.dot(feats, dv[d], preferred_element_type=F32)
        total = total + jnp.where(row == d, product, 0.0)
    total = total.reshape(8, 16, 128)
    part[...] = total[:, 0:8] + total[:, 8:16]
    src, dst = (lambda i: part.at[i]), (lambda i: got.at[i])
    send_all("space", SPACE, src, dst, ssem.at[1], rsem.at[1])
    got[me] = part[me]
    wait_all("space", SPACE, src, dst, ssem.at[1], rsem.at[1])

    hidden_pre = jnp.sum(jnp.sum(got[...], axis=0), axis=0, keepdims=True)
    hidden = leaky(hidden_pre).astype(BF).astype(F32)
    out_t = do_ref[...]
    predictions = jnp.sum(hidden * out_t, axis=1, keepdims=True)
    misfit = predictions - tg_ref[:, 0:1]
    small_ref[0] = hidden * misfit
    small_ref[1] = jnp.broadcast_to(predictions, (8, 128))
    back = jnp.sum(misfit * out_t, axis=0, keepdims=True) * slope(hidden_pre)
    bsend[...] = jnp.broadcast_to(back, (16, 128)).astype(BF)
    src, dst = (lambda i: bsend), (lambda i: bh_ref.at[i])
    send_all("space", SPACE, src, dst, ssem.at[2], rsem.at[2])
    bh_ref[me] = bsend[...]
    wait_all("space", SPACE, src, dst, ssem.at[2], rsem.at[2])

    backs = bh_ref[...].reshape(128, 128)
    row = lax.broadcasted_iota(jnp.int32, (128, 512), 0) % 16
    total = jnp.zeros((128, 512), F32)
    for d in range(16):
        product = lax.dot_general(
            backs, dv[d], (((1,), (1,)), ((), ())), preferred_element_type=F32
        )
        total = jnp.where(row == d, product, total)
    q_send[...] = total.astype(BF).reshape(8, 16, 512)
    src, dst = (lambda i: q_send.at[i]), (lambda i: b_ref.at[i])
    send_all("space", SPACE, src, dst, ssem.at[3], rsem.at[3])
    b_ref[me] = q_send[me]
    wait_all("space", SPACE, src, dst, ssem.at[3], rsem.at[3])


def dense(feats, dense_in, out_t, tg):
    return pl.pallas_call(
        dense_kernel,
        out_shape=[
            jax.ShapeDtypeStruct((8, 16, 512), BF),
            jax.ShapeDtypeStruct((8, 16, 512), BF),
            jax.ShapeDtypeStruct((8, 16, 128), BF),
            jax.ShapeDtypeStruct((2, 8, 128), F32),
        ],
        in_specs=[VM, pl.BlockSpec(memory_space=pl.ANY), VM, VM],
        out_specs=[VM] * 4,
        scratch_shapes=[
            pltpu.VMEM((16, 512, 128), BF),
            pltpu.VMEM((8, 8, 128), F32),
            pltpu.VMEM((8, 8, 128), F32),
            pltpu.VMEM((16, 128), BF),
            pltpu.VMEM((8, 16, 512), BF),
            pltpu.SemaphoreType.DMA((4, 8)),
            pltpu.SemaphoreType.DMA((4, 8)),
            pltpu.SemaphoreType.DMA((16,)),
        ],
        compiler_params=pltpu.CompilerParams(
            collective_id=3, has_side_effects=True, vmem_limit_bytes=VLIM
        ),
    )(feats, dense_in, out_t, tg)


def second_back_kernel(p_ref, x_ref, b_ref, w_ref, m_ref, sp_ref, o_ref, gw_ref, s_ref, g_ref):
    masks = m_ref[...]
    fill_second(p_ref, masks, s_ref)
    g_ref[0] = jnp.zeros((128, 256), BF)
    g_ref[17] = jnp.zeros((128, 256), BF)
    for k in range(8):
        wide = jnp.dot(
            b_ref[:, k * 64 : (k + 1) * 64], sp_ref[...], preferred_element_type=F32
        )
        for p in (2 * k, 2 * k + 1):
            g_ref[p + 1] = (wide * slope(x_ref[p])).astype(BF)
    gw_ref[...] = jnp.zeros((128, 1728), F32)

    def plane(p, carry):
        gw_ref[...] += lax.dot_general(
            g_ref[p + 1],
            s_ref[pl.ds(p, 3)].reshape(1728, 256),
            (((1,), (1,)), ((), ())),
            preferred_element_type=F32,
        )
        taps = jnp.dot(
            w_ref[...], g_ref[pl.ds(p, 3)].reshape(384, 256), preferred_element_type=F32
        )
        total = taps[256:320]
        for i in range(9):
            if i != 4:
                total = total + shifted(
                    taps[i * 64 : (i + 1) * 64], 8 - i, HALF, masks.astype(F32)
                )
        o_ref[p] = total.astype(BF)
        return carry

    lax.fori_loop(0, 16, plane, 0)


def second_back(pooled, x, b, w_back, masks, sp):
    return pl.pallas_call(
        second_back_kernel,
        out_shape=[
            jax.ShapeDtypeStruct((16, 64, 256), BF),
            jax.ShapeDtypeStruct((128, 1728), F32),
        ],
        in_specs=[VM] * 6,
        out_specs=[VM] * 2,
        scratch_shapes=[pltpu.VMEM((18, 576, 256), BF), pltpu.VMEM((18, 128, 256), BF)],
        compiler_params=pltpu.CompilerParams(vmem_limit_bytes=VLIM),
    )(pooled, x, b, w_back, masks, sp)


def active_kernel(x_ref, b_ref, st_ref, gs_ref, sp_ref, o_ref, sum_ref):
    white = (x_ref[0] - st_ref[:, 0:1]) * st_ref[:, 1:2]
    bent = slope(gs_ref[:, 0:1] * white + gs_ref[:, 1:2])
    wide = jnp.dot(b_ref[0], sp_ref[...], preferred_element_type=F32)
    wide = jnp.concatenate([wide[0:64], wide[0:64], wide[64:128], wide[64:128]], axis=0)
    active = wide * bent
    o_ref[0] = active.astype(BF)
    lane = lax.broadcasted_iota(jnp.int32, (256, 128), 1)
    grad = jnp.sum(active, axis=1, keepdims=True)
    xgrad = jnp.sum(active * white, axis=1, keepdims=True)
    tile = jnp.where(lane == 0, grad, jnp.where(lane == 1, xgrad, 0.0))

    @pl.when(pl.program_id(0) == 0)
    def _():
        sum_ref[...] = tile

    @pl.when(pl.program_id(0) > 0)
    def _():
        sum_ref[...] += tile


def back_active(x, b, st, gs, sp):
    return pl.pallas_call(
        active_kernel,
        grid=(8,),
        out_shape=[
            jax.ShapeDtypeStruct((8, 256, 1024), BF),
            jax.ShapeDtypeStruct((256, 128), F32),
        ],
        in_specs=[
            by_sample(256, 1024), by_sample(128, 256),
            whole(256, 128), whole(256, 128), whole(256, 1024),
        ],
        out_specs=[by_sample(256, 1024), whole(256, 128)],
        compiler_params=pltpu.CompilerParams(vmem_limit_bytes=VLIM),
    )(x, b, st, gs, sp)


def sums_kernel(s_ref, o_ref, own_ref, recv, ssem, rsem):
    greet("space", SPACE)
    me = lax.axis_index("space")
    own_ref[...] = (
        s_ref[0:64, :] + s_ref[64:128, :] + s_ref[128:192, :] + s_ref[192:256, :]
    )
    recv[me] = own_ref[...]
    await_greetings(SPACE - 1)
    src, dst = (lambda i: own_ref), (lambda i: recv.at[i])
    send_all("space", SPACE, src, dst, ssem, rsem)
    wait_all("space", SPACE, src, dst, ssem, rsem)
    tile = jnp.sum(recv[...], axis=0) * (1.0 / 262144)
    for p in range(4):
        o_ref[p * 64 : (p + 1) * 64, :] = tile


def group_sums(s):
    return pl.pallas_call(
        sums_kernel,
        out_shape=[jax.ShapeDtypeStruct((256, 128), F32), jax.ShapeDtypeStruct((64, 128), F32)],
        in_specs=[VM],
        out_specs=[VM] * 2,
        scratch_shapes=[
            pltpu.VMEM((8, 64, 128), F32),
            pltpu.SemaphoreType.DMA((8,)),
            pltpu.SemaphoreType.DMA((8,)),
        ],
        compiler_params=pltpu.CompilerParams(collective_id=4, has_side_effects=True),
    )(s)


def first_back_kernel(
    x_ref, a_ref, v_ref, h_ref, st_ref, gs_ref, gh_ref, m_ref, o_ref, s_ref, acc
):
    fill_first(v_ref, h_ref, m_ref[...], s_ref)
    white = (x_ref[0] - st_ref[:, 0:1]) * st_ref[:, 1:2]
    back = (gs_ref[:, 0:1] * st_ref[:, 1:2]) * (
        a_ref[0].astype(F32) - gh_ref[:, 0:1] - white * gh_ref[:, 1:2]
    )
    product = lax.dot_general(
        back.astype(BF), s_ref[...], (((1,), (1,)), ((), ())), preferred_element_type=F32
    )

    @pl.when(pl.program_id(0) == 0)
    def _():
        acc[...] = product

    @pl.when(pl.program_id(0) > 0)
    def _():
        acc[...] += product

    @pl.when(pl.program_id(0) == 7)
    def _():
        for i in range(9):
            for a in range(3):
                total = 0.0
                for p in range(4):
                    at = i * 192 + (p + a) * 32
                    total = total + acc[p * 64 : (p + 1) * 64, at : at + 32]
                o_ref[:, (a * 9 + i) * 32 : (a * 9 + i + 1) * 32] = total


def first_back(x, a, v, h, st, gs, gh, masks):
    return pl.pallas_call(
        first_back_kernel,
        grid=(8,),
        out_shape=jax.ShapeDtypeStruct((64, 864), F32),
        in_specs=[
            by_sample(256, 1024), by_sample(256, 1024), V_SPEC, H_SPEC,
            whole(256, 128), whole(256, 128), whole(256, 128), whole(9, 1024),
        ],
        out_specs=whole(64, 864),
        scratch_shapes=[pltpu.VMEM((1728, 1024), BF), pltpu.VMEM((256, 1728), F32)],
        compiler_params=pltpu.CompilerParams(vmem_limit_bytes=VLIM),
    )(x, a, v, h, st, gs, gh, masks)


LANES = 2176
TILES = LANES // 128


def reduce_kernel(
    x_ref, fx_ref, bh_ref,
    o_ref, f_ref, ba_ref,
    got1, tiles, got2, piece, got3, strip, ssem, rsem, tsem, usem,
):
    greet("space", SPACE)
    greet("dp", DP)
    me, group = lax.axis_index("space"), lax.axis_index("dp")
    await_greetings(SPACE - 1 + DP - 1)

    src1, dst1 = (lambda i: x_ref.at[i]), (lambda i: got1.at[i])
    send_all("space", SPACE, src1, dst1, ssem.at[0], rsem.at[0])
    src_f, dst_f = (lambda i: fx_ref.at[i]), (lambda i: f_ref.at[i])
    send_all("dp", DP, src_f, dst_f, tsem.at[0], usem.at[0])
    src_b, dst_b = (lambda i: bh_ref), (lambda i: ba_ref.at[i])
    send_all("dp", DP, src_b, dst_b, tsem.at[1], usem.at[1])
    f_ref[group] = fx_ref[group]
    ba_ref[group] = bh_ref[...]
    got1[me] = x_ref[me]
    tiles[TILES:32] = jnp.zeros((32 - TILES, 16, 128), F32)
    wait_all("space", SPACE, src1, dst1, ssem.at[0], rsem.at[0])
    for t in range(TILES):
        tiles[t] = jnp.sum(got1[:, :, t * 128 : (t + 1) * 128], axis=0)

    src2, dst2 = (lambda i: tiles.at[pl.ds(i * 2, 2)]), (lambda i: got2.at[i])
    send_all("dp", DP, src2, dst2, tsem.at[2], usem.at[2])
    got2[group] = tiles[pl.ds(group * 2, 2)]
    wait_all("dp", DP, src2, dst2, tsem.at[2], usem.at[2])
    piece[...] = jnp.sum(got2[...], axis=0)

    src3, dst3 = (lambda i: piece), (lambda i: got3.at[pl.ds(i * 2, 2)])
    send_all("dp", DP, src3, dst3, tsem.at[3], usem.at[3])
    got3[pl.ds(group * 2, 2)] = piece[...]
    wait_all("dp", DP, src3, dst3, tsem.at[3], usem.at[3])
    for t in range(TILES):
        strip[:, t * 128 : (t + 1) * 128] = got3[t]

    src4, dst4 = (lambda i: strip), (lambda i: o_ref.at[i])
    send_all("space", SPACE, src4, dst4, ssem.at[1], rsem.at[1])
    o_ref[me] = strip[...]
    wait_all("space", SPACE, src4, dst4, ssem.at[1], rsem.at[1])
    wait_all("dp", DP, src_f, dst_f, tsem.at[0], usem.at[0])
    wait_all("dp", DP, src_b, dst_b, tsem.at[1], usem.at[1])


def reduce_all(x, fx, bh):
    return pl.pallas_call(
        reduce_kernel,
        out_shape=[
            jax.ShapeDtypeStruct((8, 16, LANES), F32),
            jax.ShapeDtypeStruct((16, 32, 128), BF),
            jax.ShapeDtypeStruct((16, 16, 128), BF),
        ],
        in_specs=[VM] * 3,
        out_specs=[VM] * 3,
        scratch_shapes=[
            pltpu.VMEM((8, 16, LANES), F32),
            pltpu.VMEM((32, 16, 128), F32),
            pltpu.VMEM((16, 2, 16, 128), F32),
            pltpu.VMEM((2, 16, 128), F32),
            pltpu.VMEM((32, 16, 128), F32),
            pltpu.VMEM((16, LANES), F32),
            pltpu.SemaphoreType.DMA((2, 8)),
            pltpu.SemaphoreType.DMA((2, 8)),
            pltpu.SemaphoreType.DMA((4, 16)),
            pltpu.SemaphoreType.DMA((4, 16)),
        ],
        compiler_params=pltpu.CompilerParams(
            collective_id=5, has_side_effects=True, vmem_limit_bytes=VLIM
        ),
    )(x, fx, bh)


def columns_of(first, second):
    tile = jnp.stack([first, second], axis=1)
    return jnp.pad(jnp.tile(tile, (4, 1)), ((0, 0), (0, 126)))


def shards(inputs, conv_in, norm_gain, norm_shift, conv_out, dense_in, dense_out, targets):
    masks1 = jnp.asarray(shift_masks(GRID), BF)
    masks2 = jnp.asarray(shift_masks(HALF), BF)
    spread1 = jnp.asarray(spread_matrix(GRID), BF)
    spread2 = jnp.asarray(spread_matrix(HALF), BF)

    taps = conv_in.reshape(64, 3, 9, 32).transpose(0, 2, 1, 3)
    w_big = jnp.stack(
        [jnp.pad(taps, ((0, 0), (0, 0), (p, 3 - p), (0, 0))) for p in range(4)], axis=0
    ).reshape(256, 1728)
    gs = columns_of(norm_gain, norm_shift)
    w_out = conv_out.reshape(16, 8, 1728).transpose(1, 0, 2).reshape(128, 1728)
    w_back = w_out.reshape(128, 3, 9, 64)[:, ::-1].transpose(2, 3, 1, 0).reshape(576, 384)
    out_t = jnp.pad(dense_out.astype(F32).T, ((0, 4), (0, 0)))
    tg = jnp.broadcast_to(jnp.pad(targets, ((0, 0), (0, 4))).T, (8, 128))

    v = inputs.transpose(2, 0, 1, 3)
    h = halo(v)
    first_out, blocks = first_conv(v, h, w_big, masks1)
    st = stats(blocks)
    pooled = exchange(pool_first(first_out, st, gs, spread1), "space", SPACE, 6)
    pooled = pooled.reshape(1024, 256)
    second_out, feats = second_conv(pooled, w_out, masks2, spread2)
    b_feats, fx, bh, small = dense(
        feats.reshape(8, 16, 512), dense_in.reshape(16, 8, 512, 128), out_t, tg
    )
    back, grad_out = second_back(
        pooled, second_out, b_feats.reshape(128, 512), w_back, masks2, spread2
    )
    back = exchange(back.reshape(8, 128, 256), "space", SPACE, 7)
    active, sums = back_active(first_out, back, st, gs, spread1)
    gh, own = group_sums(sums)
    grad_in = first_back(first_out, active, v, h, st, gs, gh, masks1)

    packed = jnp.concatenate(
        [
            grad_out,
            jnp.concatenate([grad_in[:, :432], grad_in[:, 432:]], axis=0),
            small[0, :4].T,
            jnp.concatenate([own[:, 1:2], own[:, 0:1]], axis=0),
            jnp.zeros((128, LANES - 2165), F32),
        ],
        axis=1,
    )
    fx = fx.transpose(1, 0, 2).reshape(16, 32, 128)
    bh = jnp.pad(bh[:, 0, :], ((0, 8), (0, 0)))
    summed, f_all, bh_all = reduce_all(packed.reshape(8, 16, LANES), fx, bh)
    summed = summed.reshape(128, LANES)
    grad_conv_out = (
        summed[:, :1728].reshape(8, 16, 1728).transpose(1, 0, 2).reshape(128, 1728)
    )
    grad_conv_in = jnp.concatenate([summed[:64, 1728:2160], summed[64:, 1728:2160]], axis=1)
    grad_dense_out = summed[:, 2160:2164]
    grad_norm = summed[:, 2164].reshape(2, 64)
    grad_dense_in = lax.dot_general(
        f_all.reshape(128, 512),
        bh_all[:, :8].reshape(128, 128),
        (((0,), (0,)), ((), ())),
        preferred_element_type=F32,
    )
    predictions = small[1, :4, 0].reshape(1, 4)
    return grad_conv_in, grad_norm, grad_conv_out, grad_dense_in, grad_dense_out, predictions


def solution(mesh):
    placed = (P("dp", None, "space", None), P(), P(), P(), P(), P(), P(), P(("dp", "space"), None))
    return jax.shard_map(
        shards,
        mesh=mesh,
        in_specs=placed,
        out_specs=(P(), P(), P(), P(("dp", "space"), None), P(), P(("dp", "space"), None)),
        check_vma=False,
    )
```

```python
import functools

import jax
import jax.numpy as jnp
import numpy as np
from jax import lax
from jax.experimental import pallas as pl
from jax.experimental.pallas import tpu as pltpu
from jax.sharding import PartitionSpec as P

MESH = pl.DeviceIdType.MESH
BF = jnp.bfloat16
F32 = jnp.float32
SPACE, DP = 8, 16
GRID, HALF = 32, 16
EPS = 1e-05
WINDOW = 2
VLIM = 60 << 20

VM = pl.BlockSpec(memory_space=pltpu.VMEM)


def leaky(v):
    return v * (0.65 + 0.35 * jnp.tanh(v))


def slope(v):
    t = jnp.tanh(v)
    return 0.65 + 0.35 * (t + v * (1.0 - t * t))


def shift_masks(extent):
    rows = []
    y, z = np.divmod(np.arange(extent * extent), extent)
    for b in (-1, 0, 1):
        for d in (-1, 0, 1):
            rows.append((y + b >= 0) & (y + b < extent) & (z + d >= 0) & (z + d < extent))
    return np.stack(rows).astype(np.float32)


def spread_matrix(extent):
    y, z = np.divmod(np.arange(extent * extent), extent)
    coarse = (y // 2) * (extent // 2) + z // 2
    return (np.arange((extent // 2) ** 2)[:, None] == coarse[None, :]).astype(np.float32) * 0.125


SHIFTS = [(b, d) for b in (-1, 0, 1) for d in (-1, 0, 1)]


def shifted(block, index, extent, mask):
    b, d = SHIFTS[index]
    step = b * extent + d
    if step == 0:
        return block
    cells = extent * extent
    return pltpu.roll(block, (-step) % cells, 1) * mask[index : index + 1, :]


class Swap:
    def __init__(self, axis, sems, index, source, target):
        self.axis, self.source, self.target = axis, source, target
        self.count = SPACE if axis == "space" else DP
        self.send_sem, self.recv_sem = sems[0].at[index], sems[1].at[index]

    def copy(self, to, source, target, k):
        return pltpu.make_async_remote_copy(
            source, target, self.send_sem.at[k], self.recv_sem.at[k],
            device_id={self.axis: to}, device_id_type=MESH,
        )

    def start_one(self, k):
        me = lax.axis_index(self.axis)
        to = lax.rem(me + k, self.count)
        self.copy(to, self.source(to), self.target(me), k).start()

    def start(self):
        def send(k, carry):
            self.start_one(k)
            return carry

        lax.fori_loop(1, self.count, send, 0)

    def wait_one(self, k):
        fro = lax.rem(lax.axis_index(self.axis) + self.count - k, self.count)
        self.copy(fro, self.source(fro), self.target(fro), k).wait()

    def wait(self):
        def one(k, carry):
            self.wait_one(k)
            return carry

        lax.fori_loop(1, self.count, one, 0)


def greet(axis, count):
    me = lax.axis_index(axis)
    barrier = pltpu.get_barrier_semaphore()

    def signal(k, carry):
        pl.semaphore_signal(
            barrier, inc=1, device_id={axis: lax.rem(me + k, count)}, device_id_type=MESH
        )
        return carry

    lax.fori_loop(1, count, signal, 0)


def nt(a, b):
    return lax.dot_general(a, b, (((1,), (1,)), ((), ())), preferred_element_type=F32)


def nn(a, b):
    return jnp.dot(a, b, preferred_element_type=F32)


def nt_split(a, b):
    high = a.astype(BF)
    low = (a - high.astype(F32)).astype(BF)
    return nt(high, b) + nt(low, b)


def pick(rows, column):
    row = lax.broadcasted_iota(jnp.int32, (rows, 128), 0)
    lane = lax.broadcasted_iota(jnp.int32, (rows, 128), 1)
    return (lane == column(row)).astype(F32).astype(BF)


def two_lanes(first, second):
    lane = lax.broadcasted_iota(jnp.int32, (first.shape[0], 128), 1)
    return jnp.where(lane == 0, first, jnp.where(lane == 1, second, 0.0))


def loop(start, stop, body):
    def step(i, carry):
        body(i)
        return carry

    lax.fori_loop(start, stop, step, 0)


def block_kernel(
    v_ref, cin_ref, wt_ref, gain_ref, bias_ref, out_ref, tg_ref, d_ref, m1_ref, m2_ref, sp1_ref, sp2_ref,
    gout_ref, xout_ref, gdi_ref, pred_ref,
    fall_ref, ball_ref,
    vx, s1, f1, even, wbig, wout, wback, s2, x2, g, gwt, acc, st, gh, gs,
    stile, sgot, fsc, fsend, fx, part, pgot, bfsend, bfgot, bsc, bk,
    own, ogot, fdp, bdp, gsend, ggot, gtile, ggot2, gpiece, ggot3, xsend, xgot, xpiece, xgot2,
    xsum, dv, sp_s, sp_r, dp_s, dp_r, dsem, lsem,
):
    me, group = lax.axis_index("space"), lax.axis_index("dp")
    space, across = (sp_s, sp_r), (dp_s, dp_r)

    greet("space", SPACE)
    greet("dp", DP)
    keep = pltpu.make_async_copy(v_ref.at[me], vx.at[me], lsem)
    keep.start()

    def fetch(d):
        return pltpu.make_async_copy(d_ref.at[d, me], dv.at[d], dsem.at[d])

    for d in range(16):
        fetch(d).start()
    pl.semaphore_wait(pltpu.get_barrier_semaphore(), SPACE - 1 + DP - 1)

    slabs = Swap("space", space, 0, lambda i: v_ref.at[i], lambda i: vx.at[i])
    for k in range(1, WINDOW + 1):
        slabs.start_one(k)

    wbig[...] = jnp.zeros((256, 1728), BF)
    for p in range(4):
        wbig[p * 64 : (p + 1) * 64, p * 288 : p * 288 + 864] = cin_ref[...]
    wout[...] = nt(pick(128, lambda r: r), wt_ref[...]).astype(BF)
    for a in range(3):
        wback[:, a * 128 : (a + 1) * 128] = wt_ref[(2 - a) * 576 : (3 - a) * 576, :]
    same = lax.broadcasted_iota(jnp.int32, (64, 64), 0) == lax.broadcasted_iota(
        jnp.int32, (64, 64), 1
    )
    affine = two_lanes(
        jnp.sum(jnp.where(same, gain_ref[...], 0.0), axis=1, keepdims=True),
        jnp.sum(jnp.where(same, bias_ref[...], 0.0), axis=1, keepdims=True),
    )
    for p in range(4):
        gs[p * 64 : (p + 1) * 64, :] = affine
    s1[0] = jnp.zeros((288, 1024), BF)
    s1[33] = jnp.zeros((288, 1024), BF)
    s2[0] = jnp.zeros((576, 256), BF)
    s2[17] = jnp.zeros((576, 256), BF)
    g[0] = jnp.zeros((128, 256), BF)
    g[17] = jnp.zeros((128, 256), BF)

    def unfold_slab(s):
        masks = m1_ref[...]
        block = vx[s].reshape(128, 1024)
        for i in range(9):
            s1[pl.ds(4 * s + 1, 4), i * 32 : (i + 1) * 32, :] = shifted(
                block, i, GRID, masks
            ).reshape(4, 32, 1024)

    def taps1(s):
        return s1[pl.ds(4 * s, 6)].reshape(1728, 1024)

    def four(rows):
        return rows[0:64] + rows[64:128] + rows[128:192] + rows[192:256]

    def first_slab(s):
        out = nn(wbig[...], taps1(s))
        f1[s] = out
        total = four(jnp.sum(out, axis=1, keepdims=True))
        mean = total * (1.0 / 4096)
        off = out - jnp.concatenate([mean] * 4, axis=0)
        stile[s] = two_lanes(total, four(jnp.sum(off * off, axis=1, keepdims=True)))

    keep.wait()
    unfold_slab(me)

    def arrive(k):
        slabs.wait_one(k)

        @pl.when(k + WINDOW < SPACE)
        def _():
            slabs.start_one(k + WINDOW)

        unfold_slab(lax.rem(me + 8 - k, 8))

    loop(1, 2, arrive)

    def steady(k):
        arrive(k)
        first_slab(lax.rem(me + 9 - k, 8))

    loop(2, 8, steady)
    loop(8, 10, lambda k: first_slab(lax.rem(me + 9 - k, 8)))

    def combine(parts, cells):
        total = functools.reduce(lambda a, b: a + b, parts)
        mean = total[:, 0:1] * (1.0 / (cells * len(parts)))
        moved = 0.0
        for one in parts:
            gap = one[:, 0:1] * (1.0 / cells) - mean
            moved = moved + gap * gap
        return total[:, 0:1], mean, total[:, 1:2] + float(cells) * moved

    total, _, deviation = combine([stile[i] for i in range(8)], 4096)
    own[...] = two_lanes(total, deviation)
    lane = lax.broadcasted_iota(jnp.int32, (1, 128), 1)
    for t in range(4):
        own[0:1, :] += jnp.where(lane == 2 + t, tg_ref[0:1, t : t + 1], 0.0)
    swap = Swap("space", space, 1, lambda i: own, lambda i: sgot.at[i])
    swap.start()
    sgot[me] = own[...]
    swap.wait()
    _, mean, deviation = combine([sgot[i] for i in range(8)], 32768)
    tile = two_lanes(mean, lax.rsqrt(deviation * (1.0 / 262144) + EPS))
    for p in range(4):
        st[p * 64 : (p + 1) * 64, :] = tile

    def whitened(s):
        return (f1[s] - st[:, 0:1]) * st[:, 1:2]

    def normed(white):
        return gs[:, 0:1] * white + gs[:, 1:2]

    def pool_slab(s):
        act = leaky(normed(whitened(s)))
        pairs = jnp.concatenate(
            [act[0:64] + act[64:128], act[128:192] + act[192:256]], axis=0
        )
        pooled = nt_split(pairs, sp1_ref[...]).astype(BF)
        masks = m2_ref[...]
        for i in range(9):
            s2[pl.ds(2 * s + 1, 2), i * 64 : (i + 1) * 64, :] = shifted(
                pooled, i, HALF, masks
            ).reshape(2, 64, 256)

    loop(0, 8, pool_slab)

    def taps2(p):
        return s2[pl.ds(p, 3)].reshape(1728, 256)

    def second_pair(k):
        low = nn(wout[...], taps2(2 * k))
        high = nn(wout[...], taps2(2 * k + 1))
        x2[2 * k] = low
        x2[2 * k + 1] = high
        fsc[k] = nt_split(leaky(low) + leaky(high), sp2_ref[...]).astype(BF)

    loop(0, 8, second_pair)

    feats = jnp.concatenate([fsc[k] for k in range(8)], axis=1)
    fsend[...] = (
        nn(pick(128, lambda r: (r % 16) * 8 + r // 16), feats).astype(BF).reshape(8, 16, 512)
    )
    swap = Swap("space", space, 2, lambda i: fsend.at[i], lambda i: fx.at[i])
    swap.start()
    fx[me] = fsend[me]
    for d in range(16):
        fetch(d).wait()
    swap.wait()
    feats = fx[...].reshape(128, 512)
    row = lax.broadcasted_iota(jnp.int32, (128, 128), 0) % 16
    total = jnp.zeros((128, 128), F32)
    for d in range(16):
        total = total + jnp.where(row == d, nn(feats, dv[d]), 0.0)
    part[...] = jnp.sum(total.reshape(8, 16, 128), axis=1)
    swap = Swap("space", space, 3, lambda i: part, lambda i: pgot.at[i])
    swap.start()
    pgot[me] = part[...]

    spread = nn(pick(256, lambda r: (r % 8) * 16 + r // 16), feats)
    half = lax.broadcasted_iota(jnp.int32, (256, 256), 0) % 16 < 8
    fdp[...] = jnp.where(half, spread[:, :256], spread[:, 256:]).astype(BF).reshape(16, 16, 256)
    swap.wait()

    hidden_pre = jnp.sum(pgot[...], axis=0)
    hidden = leaky(hidden_pre).astype(BF).astype(F32)
    wanted = jnp.concatenate([sgot[i, 0:1, :] for i in range(8)], axis=0)
    mine = lax.broadcasted_iota(jnp.int32, (8, 128), 0) == me
    lane = lax.broadcasted_iota(jnp.int32, (8, 128), 1)
    back = 0.0
    predicted = jnp.zeros((8, 128), F32)
    grad_dense_out = []
    for t in range(4):
        out_t = out_ref[t : t + 1, :].astype(F32)
        prediction = jnp.sum(hidden * out_t, axis=1, keepdims=True)
        misfit = prediction - wanted[:, 2 + t : 3 + t]
        predicted = jnp.where(lane == t, prediction, predicted)
        grad_dense_out.append(
            jnp.sum(jnp.where(mine, hidden * misfit, 0.0), axis=0, keepdims=True)
        )
        back = back + misfit * out_t
    grad_dense_out = jnp.concatenate(grad_dense_out, axis=0)
    pred_ref[...] = jnp.sum(jnp.where(mine, predicted, 0.0), axis=0, keepdims=True)[:, 0:4]
    back = (back * slope(hidden_pre)).astype(BF).astype(F32)
    bdp[...] = jnp.concatenate([back, back], axis=0).astype(BF)
    backs = jnp.broadcast_to(back.reshape(8, 1, 128), (8, 16, 128)).reshape(128, 128).astype(BF)
    row = lax.broadcasted_iota(jnp.int32, (128, 512), 0) % 16
    total = jnp.zeros((128, 512), F32)
    for d in range(16):
        total = jnp.where(row == d, nt(backs, dv[d]), total)
    bfsend[...] = total.reshape(8, 16, 512)
    swap = Swap("space", space, 5, lambda i: bfsend.at[i], lambda i: bfgot.at[i])
    swap.start()
    bfgot[me] = bfsend[me]
    far_feats = Swap("dp", across, 0, lambda i: fdp.at[i], lambda i: fall_ref.at[i])
    far_feats.start()
    fall_ref[group] = fdp[group]
    far_backs = Swap("dp", across, 1, lambda i: bdp, lambda i: ball_ref.at[i])
    far_backs.start()
    ball_ref[group] = bdp[...]
    swap.wait()
    got = bfgot[...].reshape(128, 512)
    high = got.astype(BF)
    low = (got - high.astype(F32)).astype(BF)
    order = pick(128, lambda r: (r % 8) * 16 + r // 8)
    for i, one in enumerate((high, low)):
        ordered = nn(order, one).astype(BF)
        for k in range(8):
            bsc[i, k] = ordered[:, k * 64 : (k + 1) * 64]

    def back_pair(k):
        wide = nn(bsc[0, k], sp2_ref[...]) + nn(bsc[1, k], sp2_ref[...])
        g[2 * k + 1] = (wide * slope(x2[2 * k])).astype(BF)
        g[2 * k + 2] = (wide * slope(x2[2 * k + 1])).astype(BF)

    loop(0, 8, back_pair)
    gwt[...] = jnp.zeros((1728, 128), F32)

    def back_plane(p):
        gwt[...] += nt(taps2(p), g[p + 1])
        taps = nn(wback[...], g[pl.ds(p, 3)].reshape(384, 256))
        masks = m2_ref[...].astype(F32)
        total = taps[256:320]
        for i in range(9):
            if i != 4:
                total = total + shifted(taps[i * 64 : (i + 1) * 64], 8 - i, HALF, masks)
        bk[p] = total.astype(BF)

    loop(0, 16, back_plane)

    gsend[...] = jnp.concatenate(
        [gwt[...].astype(BF), jnp.zeros((320, 128), BF)], axis=0
    ).reshape(8, 256, 128)
    swap1 = Swap("space", space, 6, lambda i: gsend.at[i], lambda i: ggot.at[i])
    swap1.start()
    ggot[me] = gsend[me]

    own[...] = jnp.zeros((64, 128), F32)

    def active_of(s, white):
        wide = nn(bk[pl.ds(2 * s, 2)].reshape(128, 256), sp1_ref[...])
        wide = jnp.concatenate([wide[0:64], wide[0:64], wide[64:128], wide[64:128]], axis=0)
        return wide * slope(normed(white))

    def active_slab(s):
        white = whitened(s)
        active = active_of(s, white)
        own[...] += two_lanes(
            four(jnp.sum(active, axis=1, keepdims=True)),
            four(jnp.sum(active * white, axis=1, keepdims=True)),
        )

    loop(0, 8, active_slab)
    swap = Swap("space", space, 7, lambda i: own, lambda i: ogot.at[i])
    swap.start()
    ogot[me] = own[...]
    swap1.wait()
    gtile[...] = jnp.sum(ggot[...].astype(F32), axis=0).astype(BF).reshape(16, 16, 128)
    swap2 = Swap("dp", across, 2, lambda i: gtile.at[i], lambda i: ggot2.at[i])
    swap2.start()
    ggot2[group] = gtile[group]
    swap.wait()
    tile = jnp.sum(ogot[...], axis=0) * (1.0 / 262144)
    for p in range(4):
        gh[p * 64 : (p + 1) * 64, :] = tile
    acc[...] = jnp.zeros((256, 1728), F32)

    def first_back_slab(s):
        white = whitened(s)
        even[...] = (
            (gs[:, 0:1] * st[:, 1:2])
            * (active_of(s, white) - gh[:, 0:1] - white * gh[:, 1:2])
        ).astype(BF)
        acc[...] += nt(even[...], taps1(s))

    loop(0, 3, first_back_slab)
    far_feats.wait()
    far_backs.wait()
    backs = ball_ref[...].reshape(256, 128)
    upper = lax.broadcasted_iota(jnp.int32, (256, 128), 0) % 16 < 8
    halves = jnp.concatenate(
        [jnp.where(upper, backs, jnp.zeros_like(backs)), jnp.where(upper, jnp.zeros_like(backs), backs)],
        axis=1,
    )
    product = lax.dot_general(
        fall_ref[...].reshape(256, 256), halves, (((0,), (0,)), ((), ())),
        preferred_element_type=F32,
    )
    gdi_ref[0:256, :] = product[:, 0:128]
    gdi_ref[256:512, :] = product[:, 128:256]
    swap2.wait()
    gpiece[...] = jnp.sum(ggot2[...].astype(F32), axis=0).astype(BF)
    swap3 = Swap("dp", across, 3, lambda i: gpiece, lambda i: ggot3.at[i])
    swap3.start()
    ggot3[group] = gpiece[...]
    loop(3, 6, first_back_slab)
    swap3.wait()
    swap4 = Swap("space", space, 8, lambda i: ggot3, lambda i: gout_ref.at[i])
    swap4.start()
    gout_ref[me] = ggot3[...]
    loop(6, 8, first_back_slab)

    grad = functools.reduce(
        lambda a, b: a + b,
        [acc[p * 64 : (p + 1) * 64, p * 288 : p * 288 + 864] for p in range(4)],
    )
    xsend[...] = jnp.zeros((8, 64, 128), F32)
    for t in range(6):
        xsend[t] = grad[:, t * 128 : (t + 1) * 128]
    xsend[6, :, 0:96] = grad[:, 768:864]
    xsend[7] = own[...]
    for i in range(4):
        xsend[6, 4 * i : 4 * i + 4, 96:128] = grad_dense_out[0:4, 32 * i : 32 * i + 32]
    swap = Swap("space", space, 9, lambda i: xsend.at[i], lambda i: xgot.at[i])
    swap.start()
    xgot[me] = xsend[me]
    swap.wait()
    xpiece[...] = jnp.sum(xgot[...], axis=0).astype(BF)
    swap = Swap("dp", across, 4, lambda i: xpiece, lambda i: xgot2.at[i])
    swap.start()
    xgot2[group] = xpiece[...]
    swap.wait()
    xsum[...] = jnp.sum(xgot2[...].astype(F32), axis=0).astype(BF)
    swap = Swap("space", space, 10, lambda i: xsum, lambda i: xout_ref.at[i])
    swap.start()
    xout_ref[me] = xsum[...]
    swap4.wait()
    swap.wait()


def finish_kernel(
    gout_ref, xout_ref, gdi_in_ref, pred_in_ref,
    gci_ref, gnorm_ref, gco_ref, gdi_ref, gdo_ref, pred_ref,
):
    gco_ref[...] = gout_ref[...].reshape(2048, 128)[0:1728].astype(F32)
    gdi_ref[...] = gdi_in_ref[...]
    pred_ref[...] = pred_in_ref[...]
    for t in range(6):
        gci_ref[:, t * 128 : (t + 1) * 128] = xout_ref[t].astype(F32)
    last = xout_ref[6].astype(F32)
    gci_ref[:, 768:864] = last[:, 0:96]
    for i in range(4):
        gdo_ref[:, 32 * i : 32 * i + 32] = last[4 * i : 4 * i + 4, 96:128]
    sums = xout_ref[7].astype(F32).T
    gnorm_ref[...] = jnp.concatenate([sums[1:2, :], sums[0:1, :]], axis=0)


def finish(gout, xout, gdi, pred):
    return pl.pallas_call(
        finish_kernel,
        out_shape=[
            jax.ShapeDtypeStruct(shape, F32)
            for shape in ((64, 864), (2, 64), (1728, 128), (512, 128), (4, 128), (1, 4))
        ],
        in_specs=[VM] * 4,
        out_specs=[VM] * 6,
        compiler_params=pltpu.CompilerParams(vmem_limit_bytes=16 << 20),
    )(gout, xout, gdi, pred)


def block(v, cin, wt, gain, bias, out_t, targets, dense_in, masks1, masks2, spread1, spread2):
    anywhere = pl.BlockSpec(memory_space=pl.ANY)
    scratch = [
        ((16, 16, 256), BF), ((16, 16, 128), BF),
        ((8, 4, 32, 1024), BF), ((34, 288, 1024), BF), ((8, 256, 1024), F32),
        ((256, 1024), BF), ((256, 1728), BF), ((128, 1728), BF), ((576, 384), BF),
        ((18, 576, 256), BF), ((16, 128, 256), F32), ((18, 128, 256), BF),
        ((1728, 128), F32), ((256, 1728), F32), ((256, 128), F32), ((256, 128), F32),
        ((256, 128), F32),
        ((8, 64, 128), F32), ((8, 64, 128), F32), ((8, 128, 64), BF), ((8, 16, 512), BF),
        ((8, 16, 512), BF), ((8, 128), F32), ((8, 8, 128), F32), ((8, 16, 512), F32), ((8, 16, 512), F32), ((2, 8, 128, 64), BF),
        ((16, 64, 256), BF),
        ((64, 128), F32), ((8, 64, 128), F32), ((16, 16, 256), BF), ((16, 128), BF),
        ((8, 256, 128), BF), ((8, 256, 128), BF), ((16, 16, 128), BF), ((16, 16, 128), BF),
        ((16, 128), BF), ((16, 16, 128), BF), ((8, 64, 128), F32), ((8, 64, 128), F32),
        ((64, 128), BF), ((16, 64, 128), BF), ((64, 128), BF), ((16, 512, 128), BF),
    ]
    return pl.pallas_call(
        block_kernel,
        out_shape=[
            jax.ShapeDtypeStruct((8, 16, 16, 128), BF),
            jax.ShapeDtypeStruct((8, 64, 128), BF),
            jax.ShapeDtypeStruct((512, 128), F32),
            jax.ShapeDtypeStruct((1, 4), F32),
        ],
        in_specs=[anywhere] + [VM] * 6 + [anywhere] + [VM] * 4,
        out_specs=[VM] * 4,
        scratch_shapes=[pltpu.VMEM(shape, kind) for shape, kind in scratch]
        + [
            pltpu.SemaphoreType.DMA((11, 8)), pltpu.SemaphoreType.DMA((11, 8)),
            pltpu.SemaphoreType.DMA((5, 16)), pltpu.SemaphoreType.DMA((5, 16)),
            pltpu.SemaphoreType.DMA((16,)), pltpu.SemaphoreType.DMA,
        ],
        compiler_params=pltpu.CompilerParams(
            collective_id=1, has_side_effects=True, vmem_limit_bytes=VLIM
        ),
    )(v, cin, wt, gain, bias, out_t, targets, dense_in, masks1, masks2, spread1, spread2)


def shards(inputs, conv_in, norm_gain, norm_shift, conv_out, dense_in, dense_out, targets):
    masks1 = jnp.asarray(shift_masks(GRID), BF)
    masks2 = jnp.asarray(shift_masks(HALF), BF)
    spread1 = jnp.asarray(spread_matrix(GRID), BF)
    spread2 = jnp.asarray(spread_matrix(HALF), BF)
    v = inputs.transpose(0, 2, 1, 3)
    parts = block(
        v, conv_in, conv_out.T, norm_gain.reshape(1, 64), norm_shift.reshape(1, 64),
        dense_out.T, targets, dense_in.reshape(16, 8, 512, 128),
        masks1, masks2, spread1, spread2,
    )
    grad_in, grad_norm, grad_out, grad_dense, grad_last, predictions = finish(*parts)
    return grad_in, grad_norm, grad_out.T, grad_dense, grad_last.T, predictions


def solution(mesh):
    placed = (P("dp", None, "space", None), P(), P(), P(), P(), P(), P(), P(("dp", "space"), None))
    return jax.shard_map(
        shards,
        mesh=mesh,
        in_specs=placed,
        out_specs=(P(), P(), P(), P(("dp", "space"), None), P(), P(("dp", "space"), None)),
        check_vma=False,
    )
```

```python
import functools

import jax
import jax.numpy as jnp
import numpy as np
from jax import lax
from jax.experimental import pallas as pl
from jax.experimental.pallas import tpu as pltpu
from jax.sharding import PartitionSpec as P

MESH = pl.DeviceIdType.MESH
BF = jnp.bfloat16
F32 = jnp.float32
SPACE, DP = 8, 16
GRID, HALF = 32, 16
EPS = 1e-05
WINDOW = 2
VLIM = 60 << 20

VM = pl.BlockSpec(memory_space=pltpu.VMEM)


def leaky(v):
    return v * (0.65 + 0.35 * jnp.tanh(v))


def slope(v):
    t = jnp.tanh(v)
    return 0.65 + 0.35 * (t + v * (1.0 - t * t))


def shift_masks(extent):
    rows = []
    y, z = np.divmod(np.arange(extent * extent), extent)
    for b in (-1, 0, 1):
        for d in (-1, 0, 1):
            rows.append((y + b >= 0) & (y + b < extent) & (z + d >= 0) & (z + d < extent))
    return np.stack(rows).astype(np.float32)


def spread_matrix(extent):
    y, z = np.divmod(np.arange(extent * extent), extent)
    coarse = (y // 2) * (extent // 2) + z // 2
    return (np.arange((extent // 2) ** 2)[:, None] == coarse[None, :]).astype(np.float32) * 0.125


SHIFTS = [(b, d) for b in (-1, 0, 1) for d in (-1, 0, 1)]


def shifted(block, index, extent, mask):
    b, d = SHIFTS[index]
    step = b * extent + d
    if step == 0:
        return block
    cells = extent * extent
    return pltpu.roll(block, (-step) % cells, 1) * mask[index : index + 1, :]


class Swap:
    def __init__(self, axis, sems, index, source, target):
        self.axis, self.source, self.target = axis, source, target
        self.count = SPACE if axis == "space" else DP
        self.send_sem, self.recv_sem = sems[0].at[index], sems[1].at[index]

    def copy(self, to, source, target, k):
        return pltpu.make_async_remote_copy(
            source, target, self.send_sem.at[k], self.recv_sem.at[k],
            device_id={self.axis: to}, device_id_type=MESH,
        )

    def start_one(self, k):
        me = lax.axis_index(self.axis)
        to = lax.rem(me + k, self.count)
        self.copy(to, self.source(to), self.target(me), k).start()

    def start(self):
        def send(k, carry):
            self.start_one(k)
            return carry

        lax.fori_loop(1, self.count, send, 0)

    def wait_one(self, k):
        fro = lax.rem(lax.axis_index(self.axis) + self.count - k, self.count)
        self.copy(fro, self.source(fro), self.target(fro), k).wait()

    def wait(self):
        def one(k, carry):
            self.wait_one(k)
            return carry

        lax.fori_loop(1, self.count, one, 0)


def greet(axis, count):
    me = lax.axis_index(axis)
    barrier = pltpu.get_barrier_semaphore()

    def signal(k, carry):
        pl.semaphore_signal(
            barrier, inc=1, device_id={axis: lax.rem(me + k, count)}, device_id_type=MESH
        )
        return carry

    lax.fori_loop(1, count, signal, 0)


def nt(a, b):
    return lax.dot_general(a, b, (((1,), (1,)), ((), ())), preferred_element_type=F32)


def nn(a, b):
    return jnp.dot(a, b, preferred_element_type=F32)


def nt_split(a, b):
    high = a.astype(BF)
    low = (a - high.astype(F32)).astype(BF)
    return nt(high, b) + nt(low, b)


def pick(rows, column):
    row = lax.broadcasted_iota(jnp.int32, (rows, 128), 0)
    lane = lax.broadcasted_iota(jnp.int32, (rows, 128), 1)
    return (lane == column(row)).astype(F32).astype(BF)


def two_lanes(first, second):
    lane = lax.broadcasted_iota(jnp.int32, (first.shape[0], 128), 1)
    return jnp.where(lane == 0, first, jnp.where(lane == 1, second, 0.0))


def loop(start, stop, body):
    def step(i, carry):
        body(i)
        return carry

    lax.fori_loop(start, stop, step, 0)


def block_kernel(
    v_ref, cin_ref, wt_ref, gain_ref, bias_ref, out_ref, tg_ref, d_ref, m1_ref, m2_ref, sp1_ref, sp2_ref,
    sums_ref, gdi_ref,
    fall_ref, ball_ref,
    vx, s1, f1, even, wbig, wout, wback, s2, x2, g, gwt, acc, st, gh, gs,
    stile, sgot, fsc, fsend, fx, part, pgot, bfsend, bfgot, bsc, bk,
    own, ogot, fdp, bdp, gsend, ggot, gtile, ggot2, gpiece, ggot3, xsend, xgot, xpiece, xgot2,
    xsum, dv, sp_s, sp_r, dp_s, dp_r, dsem, lsem,
):
    me, group = lax.axis_index("space"), lax.axis_index("dp")
    space, across = (sp_s, sp_r), (dp_s, dp_r)

    greet("space", SPACE)
    greet("dp", DP)
    keep = pltpu.make_async_copy(v_ref.at[me], vx.at[me], lsem)
    keep.start()

    def fetch(d):
        return pltpu.make_async_copy(d_ref.at[d, me], dv.at[d], dsem.at[d])

    for d in range(16):
        fetch(d).start()
    pl.semaphore_wait(pltpu.get_barrier_semaphore(), SPACE - 1 + DP - 1)

    slabs = Swap("space", space, 0, lambda i: v_ref.at[i], lambda i: vx.at[i])
    for k in range(1, WINDOW + 1):
        slabs.start_one(k)

    wbig[...] = jnp.zeros((256, 1728), BF)
    for p in range(4):
        wbig[p * 64 : (p + 1) * 64, p * 288 : p * 288 + 864] = cin_ref[...]
    wout[...] = nt(pick(128, lambda r: r), wt_ref[...]).astype(BF)
    for a in range(3):
        wback[:, a * 128 : (a + 1) * 128] = wt_ref[(2 - a) * 576 : (3 - a) * 576, :]
    same = lax.broadcasted_iota(jnp.int32, (64, 64), 0) == lax.broadcasted_iota(
        jnp.int32, (64, 64), 1
    )
    affine = two_lanes(
        jnp.sum(jnp.where(same, gain_ref[...], 0.0), axis=1, keepdims=True),
        jnp.sum(jnp.where(same, bias_ref[...], 0.0), axis=1, keepdims=True),
    )
    for p in range(4):
        gs[p * 64 : (p + 1) * 64, :] = affine
    s1[0] = jnp.zeros((288, 1024), BF)
    s1[33] = jnp.zeros((288, 1024), BF)
    s2[0] = jnp.zeros((576, 256), BF)
    s2[17] = jnp.zeros((576, 256), BF)
    g[0] = jnp.zeros((128, 256), BF)
    g[17] = jnp.zeros((128, 256), BF)

    def unfold_slab(s):
        masks = m1_ref[...]
        block = vx[s].reshape(128, 1024)
        for i in range(9):
            s1[pl.ds(4 * s + 1, 4), i * 32 : (i + 1) * 32, :] = shifted(
                block, i, GRID, masks
            ).reshape(4, 32, 1024)

    def taps1(s):
        return s1[pl.ds(4 * s, 6)].reshape(1728, 1024)

    def four(rows):
        return rows[0:64] + rows[64:128] + rows[128:192] + rows[192:256]

    def first_slab(s):
        out = nn(wbig[...], taps1(s))
        f1[s] = out
        total = four(jnp.sum(out, axis=1, keepdims=True))
        mean = total * (1.0 / 4096)
        off = out - jnp.concatenate([mean] * 4, axis=0)
        stile[s] = two_lanes(total, four(jnp.sum(off * off, axis=1, keepdims=True)))

    keep.wait()
    unfold_slab(me)

    def arrive(k):
        slabs.wait_one(k)

        @pl.when(k + WINDOW < SPACE)
        def _():
            slabs.start_one(k + WINDOW)

        unfold_slab(lax.rem(me + 8 - k, 8))

    loop(1, 2, arrive)

    def steady(k):
        arrive(k)
        first_slab(lax.rem(me + 9 - k, 8))

    loop(2, 8, steady)
    loop(8, 10, lambda k: first_slab(lax.rem(me + 9 - k, 8)))

    def combine(parts, cells):
        total = functools.reduce(lambda a, b: a + b, parts)
        mean = total[:, 0:1] * (1.0 / (cells * len(parts)))
        moved = 0.0
        for one in parts:
            gap = one[:, 0:1] * (1.0 / cells) - mean
            moved = moved + gap * gap
        return total[:, 0:1], mean, total[:, 1:2] + float(cells) * moved

    total, _, deviation = combine([stile[i] for i in range(8)], 4096)
    own[...] = two_lanes(total, deviation)
    lane = lax.broadcasted_iota(jnp.int32, (1, 128), 1)
    for t in range(4):
        own[0:1, :] += jnp.where(lane == 2 + t, tg_ref[0:1, t : t + 1], 0.0)
    swap = Swap("space", space, 1, lambda i: own, lambda i: sgot.at[i])
    swap.start()
    sgot[me] = own[...]
    swap.wait()
    _, mean, deviation = combine([sgot[i] for i in range(8)], 32768)
    tile = two_lanes(mean, lax.rsqrt(deviation * (1.0 / 262144) + EPS))
    for p in range(4):
        st[p * 64 : (p + 1) * 64, :] = tile

    def whitened(s):
        return (f1[s] - st[:, 0:1]) * st[:, 1:2]

    def normed(white):
        return gs[:, 0:1] * white + gs[:, 1:2]

    def pool_slab(s):
        act = leaky(normed(whitened(s)))
        pairs = jnp.concatenate(
            [act[0:64] + act[64:128], act[128:192] + act[192:256]], axis=0
        )
        pooled = nt_split(pairs, sp1_ref[...]).astype(BF)
        masks = m2_ref[...]
        for i in range(9):
            s2[pl.ds(2 * s + 1, 2), i * 64 : (i + 1) * 64, :] = shifted(
                pooled, i, HALF, masks
            ).reshape(2, 64, 256)

    loop(0, 8, pool_slab)

    def taps2(p):
        return s2[pl.ds(p, 3)].reshape(1728, 256)

    def second_pair(k):
        low = nn(wout[...], taps2(2 * k))
        high = nn(wout[...], taps2(2 * k + 1))
        x2[2 * k] = low
        x2[2 * k + 1] = high
        fsc[k] = nt_split(leaky(low) + leaky(high), sp2_ref[...]).astype(BF)

    loop(0, 8, second_pair)

    feats = jnp.concatenate([fsc[k] for k in range(8)], axis=1)
    fsend[...] = (
        nn(pick(128, lambda r: (r % 16) * 8 + r // 16), feats).astype(BF).reshape(8, 16, 512)
    )
    swap = Swap("space", space, 2, lambda i: fsend.at[i], lambda i: fx.at[i])
    swap.start()
    fx[me] = fsend[me]
    for d in range(16):
        fetch(d).wait()
    swap.wait()
    feats = fx[...].reshape(128, 512)
    row = lax.broadcasted_iota(jnp.int32, (128, 128), 0) % 16
    total = jnp.zeros((128, 128), F32)
    for d in range(16):
        total = total + jnp.where(row == d, nn(feats, dv[d]), 0.0)
    part[...] = jnp.sum(total.reshape(8, 16, 128), axis=1)
    swap = Swap("space", space, 3, lambda i: part, lambda i: pgot.at[i])
    swap.start()
    pgot[me] = part[...]

    spread = nn(pick(256, lambda r: (r % 8) * 16 + r // 16), feats)
    half = lax.broadcasted_iota(jnp.int32, (256, 256), 0) % 16 < 8
    fdp[...] = jnp.where(half, spread[:, :256], spread[:, 256:]).astype(BF).reshape(16, 16, 256)
    swap.wait()

    hidden_pre = jnp.sum(pgot[...], axis=0)
    hidden = leaky(hidden_pre).astype(BF).astype(F32)
    wanted = jnp.concatenate([sgot[i, 0:1, :] for i in range(8)], axis=0)
    mine = lax.broadcasted_iota(jnp.int32, (8, 128), 0) == me
    lane = lax.broadcasted_iota(jnp.int32, (8, 128), 1)
    back = 0.0
    predicted = jnp.zeros((8, 128), F32)
    grad_dense_out = []
    for t in range(4):
        out_t = out_ref[t : t + 1, :].astype(F32)
        prediction = jnp.sum(hidden * out_t, axis=1, keepdims=True)
        misfit = prediction - wanted[:, 2 + t : 3 + t]
        predicted = jnp.where(lane == t, prediction, predicted)
        grad_dense_out.append(
            jnp.sum(jnp.where(mine, hidden * misfit, 0.0), axis=0, keepdims=True)
        )
        back = back + misfit * out_t
    grad_dense_out = jnp.concatenate(grad_dense_out, axis=0)
    gdi_ref[512:520, :] = jnp.broadcast_to(
        jnp.sum(jnp.where(mine, predicted, 0.0), axis=0, keepdims=True), (8, 128)
    )
    back = (back * slope(hidden_pre)).astype(BF).astype(F32)
    bdp[...] = jnp.concatenate([back, back], axis=0).astype(BF)
    backs = jnp.broadcast_to(back.reshape(8, 1, 128), (8, 16, 128)).reshape(128, 128).astype(BF)
    row = lax.broadcasted_iota(jnp.int32, (128, 512), 0) % 16
    total = jnp.zeros((128, 512), F32)
    for d in range(16):
        total = jnp.where(row == d, nt(backs, dv[d]), total)
    bfsend[...] = total.reshape(8, 16, 512)
    swap = Swap("space", space, 5, lambda i: bfsend.at[i], lambda i: bfgot.at[i])
    swap.start()
    bfgot[me] = bfsend[me]
    far_feats = Swap("dp", across, 0, lambda i: fdp.at[i], lambda i: fall_ref.at[i])
    far_feats.start()
    fall_ref[group] = fdp[group]
    far_backs = Swap("dp", across, 1, lambda i: bdp, lambda i: ball_ref.at[i])
    far_backs.start()
    ball_ref[group] = bdp[...]
    swap.wait()
    got = bfgot[...].reshape(128, 512)
    high = got.astype(BF)
    low = (got - high.astype(F32)).astype(BF)
    order = pick(128, lambda r: (r % 8) * 16 + r // 8)
    for i, one in enumerate((high, low)):
        ordered = nn(order, one).astype(BF)
        for k in range(8):
            bsc[i, k] = ordered[:, k * 64 : (k + 1) * 64]

    def back_pair(k):
        wide = nn(bsc[0, k], sp2_ref[...]) + nn(bsc[1, k], sp2_ref[...])
        g[2 * k + 1] = (wide * slope(x2[2 * k])).astype(BF)
        g[2 * k + 2] = (wide * slope(x2[2 * k + 1])).astype(BF)

    loop(0, 8, back_pair)
    gwt[...] = jnp.zeros((1728, 128), F32)

    def back_plane(p):
        gwt[...] += nt(taps2(p), g[p + 1])
        taps = nn(wback[...], g[pl.ds(p, 3)].reshape(384, 256))
        masks = m2_ref[...].astype(F32)
        total = taps[256:320]
        for i in range(9):
            if i != 4:
                total = total + shifted(taps[i * 64 : (i + 1) * 64], 8 - i, HALF, masks)
        bk[p] = total.astype(BF)

    loop(0, 16, back_plane)

    gsend[...] = jnp.concatenate(
        [gwt[...].astype(BF), jnp.zeros((320, 128), BF)], axis=0
    ).reshape(8, 256, 128)
    swap1 = Swap("space", space, 6, lambda i: gsend.at[i], lambda i: ggot.at[i])
    swap1.start()
    ggot[me] = gsend[me]

    own[...] = jnp.zeros((64, 128), F32)

    def active_of(s, white):
        wide = nn(bk[pl.ds(2 * s, 2)].reshape(128, 256), sp1_ref[...])
        wide = jnp.concatenate([wide[0:64], wide[0:64], wide[64:128], wide[64:128]], axis=0)
        return wide * slope(normed(white))

    def active_slab(s):
        white = whitened(s)
        active = active_of(s, white)
        own[...] += two_lanes(
            four(jnp.sum(active, axis=1, keepdims=True)),
            four(jnp.sum(active * white, axis=1, keepdims=True)),
        )

    loop(0, 8, active_slab)
    swap = Swap("space", space, 7, lambda i: own, lambda i: ogot.at[i])
    swap.start()
    ogot[me] = own[...]
    swap1.wait()
    gtile[...] = jnp.sum(ggot[...].astype(F32), axis=0).astype(BF).reshape(16, 16, 128)
    swap2 = Swap("dp", across, 2, lambda i: gtile.at[i], lambda i: ggot2.at[i])
    swap2.start()
    ggot2[group] = gtile[group]
    swap.wait()
    tile = jnp.sum(ogot[...], axis=0) * (1.0 / 262144)
    for p in range(4):
        gh[p * 64 : (p + 1) * 64, :] = tile
    acc[...] = jnp.zeros((256, 1728), F32)

    def first_back_slab(s):
        white = whitened(s)
        even[...] = (
            (gs[:, 0:1] * st[:, 1:2])
            * (active_of(s, white) - gh[:, 0:1] - white * gh[:, 1:2])
        ).astype(BF)
        acc[...] += nt(even[...], taps1(s))

    loop(0, 3, first_back_slab)
    far_feats.wait()
    far_backs.wait()
    backs = ball_ref[...].reshape(256, 128)
    upper = lax.broadcasted_iota(jnp.int32, (256, 128), 0) % 16 < 8
    halves = jnp.concatenate(
        [jnp.where(upper, backs, jnp.zeros_like(backs)), jnp.where(upper, jnp.zeros_like(backs), backs)],
        axis=1,
    )
    product = lax.dot_general(
        fall_ref[...].reshape(256, 256), halves, (((0,), (0,)), ((), ())),
        preferred_element_type=F32,
    )
    gdi_ref[0:256, :] = product[:, 0:128]
    gdi_ref[256:512, :] = product[:, 128:256]
    swap2.wait()
    gpiece[...] = jnp.sum(ggot2[...].astype(F32), axis=0).astype(BF)
    swap3 = Swap("dp", across, 3, lambda i: gpiece, lambda i: ggot3.at[i])
    swap3.start()
    ggot3[group] = gpiece[...]
    loop(3, 6, first_back_slab)
    swap3.wait()
    swap4 = Swap("space", space, 8, lambda i: ggot3, lambda i: sums_ref.at[i, pl.ds(0, 16)])
    swap4.start()
    sums_ref[me, 0:16] = ggot3[...]
    loop(6, 8, first_back_slab)

    grad = functools.reduce(
        lambda a, b: a + b,
        [acc[p * 64 : (p + 1) * 64, p * 288 : p * 288 + 864] for p in range(4)],
    )
    xsend[...] = jnp.zeros((8, 64, 128), F32)
    for t in range(6):
        xsend[t] = grad[:, t * 128 : (t + 1) * 128]
    xsend[6, :, 0:96] = grad[:, 768:864]
    xsend[7] = own[...]
    for i in range(4):
        xsend[6, 4 * i : 4 * i + 4, 96:128] = grad_dense_out[0:4, 32 * i : 32 * i + 32]
    swap = Swap("space", space, 9, lambda i: xsend.at[i], lambda i: xgot.at[i])
    swap.start()
    xgot[me] = xsend[me]
    swap.wait()
    xpiece[...] = jnp.sum(xgot[...], axis=0).astype(BF)
    swap = Swap("dp", across, 4, lambda i: xpiece, lambda i: xgot2.at[i])
    swap.start()
    xgot2[group] = xpiece[...]
    swap.wait()
    xsum[...] = jnp.sum(xgot2[...].astype(F32), axis=0).astype(BF).reshape(4, 16, 128)
    swap = Swap("space", space, 10, lambda i: xsum, lambda i: sums_ref.at[i, pl.ds(16, 4)])
    swap.start()
    sums_ref[me, 16:20] = xsum[...]
    swap4.wait()
    swap.wait()


def finish_kernel(
    sums_ref, dense_ref,
    gci_ref, gnorm_ref, gco_ref, gdi_ref, gdo_ref, pred_ref,
):
    gco_ref[...] = sums_ref[:, 0:16].reshape(2048, 128)[0:1728].astype(F32)
    gdi_ref[...] = dense_ref[0:512, :]
    pred_ref[...] = dense_ref[512:513, 0:4]

    def small(t):
        return sums_ref[t, 16:20].reshape(64, 128).astype(F32)

    for t in range(6):
        gci_ref[:, t * 128 : (t + 1) * 128] = small(t)
    last = small(6)
    gci_ref[:, 768:864] = last[:, 0:96]
    for i in range(4):
        gdo_ref[:, 32 * i : 32 * i + 32] = last[4 * i : 4 * i + 4, 96:128]
    sums = small(7).T
    gnorm_ref[...] = jnp.concatenate([sums[1:2, :], sums[0:1, :]], axis=0)


def finish(sums, dense_parts):
    return pl.pallas_call(
        finish_kernel,
        out_shape=[
            jax.ShapeDtypeStruct(shape, F32)
            for shape in ((64, 864), (2, 64), (1728, 128), (512, 128), (4, 128), (1, 4))
        ],
        in_specs=[VM] * 2,
        out_specs=[VM] * 6,
        compiler_params=pltpu.CompilerParams(vmem_limit_bytes=16 << 20),
    )(sums, dense_parts)


def block(v, cin, wt, gain, bias, out_t, targets, dense_in, masks1, masks2, spread1, spread2):
    anywhere = pl.BlockSpec(memory_space=pl.ANY)
    scratch = [
        ((16, 16, 256), BF), ((16, 16, 128), BF),
        ((8, 4, 32, 1024), BF), ((34, 288, 1024), BF), ((8, 256, 1024), F32),
        ((256, 1024), BF), ((256, 1728), BF), ((128, 1728), BF), ((576, 384), BF),
        ((18, 576, 256), BF), ((16, 128, 256), F32), ((18, 128, 256), BF),
        ((1728, 128), F32), ((256, 1728), F32), ((256, 128), F32), ((256, 128), F32),
        ((256, 128), F32),
        ((8, 64, 128), F32), ((8, 64, 128), F32), ((8, 128, 64), BF), ((8, 16, 512), BF),
        ((8, 16, 512), BF), ((8, 128), F32), ((8, 8, 128), F32), ((8, 16, 512), F32), ((8, 16, 512), F32), ((2, 8, 128, 64), BF),
        ((16, 64, 256), BF),
        ((64, 128), F32), ((8, 64, 128), F32), ((16, 16, 256), BF), ((16, 128), BF),
        ((8, 256, 128), BF), ((8, 256, 128), BF), ((16, 16, 128), BF), ((16, 16, 128), BF),
        ((16, 128), BF), ((16, 16, 128), BF), ((8, 64, 128), F32), ((8, 64, 128), F32),
        ((64, 128), BF), ((16, 64, 128), BF), ((4, 16, 128), BF), ((16, 512, 128), BF),
    ]
    return pl.pallas_call(
        block_kernel,
        out_shape=[
            jax.ShapeDtypeStruct((8, 20, 16, 128), BF),
            jax.ShapeDtypeStruct((520, 128), F32),
        ],
        in_specs=[anywhere] + [VM] * 6 + [anywhere] + [VM] * 4,
        out_specs=[VM] * 2,
        scratch_shapes=[pltpu.VMEM(shape, kind) for shape, kind in scratch]
        + [
            pltpu.SemaphoreType.DMA((11, 8)), pltpu.SemaphoreType.DMA((11, 8)),
            pltpu.SemaphoreType.DMA((5, 16)), pltpu.SemaphoreType.DMA((5, 16)),
            pltpu.SemaphoreType.DMA((16,)), pltpu.SemaphoreType.DMA,
        ],
        compiler_params=pltpu.CompilerParams(
            collective_id=1, has_side_effects=True, vmem_limit_bytes=VLIM
        ),
    )(v, cin, wt, gain, bias, out_t, targets, dense_in, masks1, masks2, spread1, spread2)


def shards(inputs, conv_in, norm_gain, norm_shift, conv_out, dense_in, dense_out, targets):
    masks1 = jnp.asarray(shift_masks(GRID), BF)
    masks2 = jnp.asarray(shift_masks(HALF), BF)
    spread1 = jnp.asarray(spread_matrix(GRID), BF)
    spread2 = jnp.asarray(spread_matrix(HALF), BF)
    v = inputs.transpose(0, 2, 1, 3)
    parts = block(
        v, conv_in, conv_out.T, norm_gain.reshape(1, 64), norm_shift.reshape(1, 64),
        dense_out.T, targets, dense_in.reshape(16, 8, 512, 128),
        masks1, masks2, spread1, spread2,
    )
    grad_in, grad_norm, grad_out, grad_dense, grad_last, predictions = finish(*parts)
    return grad_in, grad_norm, grad_out.T, grad_dense, grad_last.T, predictions


def solution(mesh):
    placed = (P("dp", None, "space", None), P(), P(), P(), P(), P(), P(), P(("dp", "space"), None))
    return jax.shard_map(
        shards,
        mesh=mesh,
        in_specs=placed,
        out_specs=(P(), P(), P(), P(("dp", "space"), None), P(), P(("dp", "space"), None)),
        check_vma=False,
    )
```
